256 devices in a mesh: lat: 32 (over z, x), lev: 8 (over y, core).
Axes of the slice: x: 4, y: 4, z: 8, core: 2. Of those that a mesh axis runs over, the one named last changes fastest.
Arguments:
- coeffs: bfloat16 [24, 2, 512, 1152], P(None, None, ('lat', 'lev')), may hold values from -12 to 12
- legendre: bfloat16 [512, 1152, 1280], P(('lat', 'lev')), may hold values from -0.1875 to 0.1875
- pair_first: int32 [512], replicated, may hold values from 0 to 511, each once
- row_counts: int32 [2560], replicated, may hold values from 20 to 5136, as said below
- quad_weights: float32 [1280], replicated, may hold values from 0.5 to 2
Outputs:
- flux_spectra: bfloat16 [16, 2, 512, 1152], P(None, None, ('lat', 'lev'))
The draws below stay inside these ranges and needn't reach their ends.
Inputs may be any that keep to these rules, and one draw needn't show every extreme that they name: row_counts[i] is a multiple of 4 within 12 of 20 + 4 min(i, 2559 - i); the two polar rows hold 20 and the two rows beside the equator 5136.
All inputs are finite; a program needn't handle non-finite values.
Results may differ from the reference program's by a relative error of at most 0.0075.
Values may be sent and summed in bfloat16 or wider, within the bound.
A program may use at most 128 MiB of HBM per device.

```python
import math
import jax
import jax.numpy as jnp
from jax import lax

WAVES = 1024
HLAT = 1280
LEVELS = 8
NLAT = 2560
NLON = 5136
PAIRS = 512
PAIRLEN = 1152
KIN = 24
KOUT = 16


def draw_row_counts(key, part):
    key = jax.random.fold_in(key, 11)
    latitude = jnp.arange(NLAT, dtype=jnp.int32)
    distance = jnp.minimum(latitude, NLAT - 1 - latitude)
    jitter = jax.random.randint(key, (NLAT,), -3, 4, dtype=jnp.int32)
    counts = jnp.clip(20 + 4 * distance + 4 * jitter, 20, NLON)
    counts = jnp.where(distance == 0, 20, counts)
    counts = jnp.where(distance == HLAT - 1, NLON, counts)
    return counts.astype(jnp.int32)


def steps_of(own_key, dims, split, smallest, high):
    factor_of = 1.0
    for position, parts in split:
        heights = jax.random.uniform(jax.random.fold_in(jax.random.fold_in(own_key, 6), position), (parts,), jnp.float32, smallest / len(split), high / len(split))
        factor_of = factor_of * jnp.repeat(jnp.exp(heights), dims[position] // parts).reshape((-1,) + (1,) * (len(dims) - 1 - position))
    return factor_of


def gaussian(stream_key, dims, deviation, limit, shards=(), held_as=jnp.bfloat16):
    array = deviation * jax.random.normal(stream_key, dims, jnp.float32)
    if shards:
        array = array * steps_of(stream_key, dims, shards, -0.22, 0.18)
    return jnp.clip(array, -limit, limit).astype(held_as)


def setup_inputs(seed: int = 0) -> dict:
    streams_of = jax.random.split(jax.random.key(seed), 6)
    coeffs = gaussian(streams_of[0], (KIN, 2, PAIRS, PAIRLEN), 2.0, 12.0, ((2, 256),))
    legendre = gaussian(streams_of[1], (PAIRS, PAIRLEN, HLAT), WAVES ** -0.5, 0.1875, ((0, 256),))
    pair_first = jax.random.permutation(streams_of[2], PAIRS).astype(jnp.int32)
    row_counts = draw_row_counts(jax.random.fold_in(streams_of[5], 71), 0)
    quad_weights = jnp.clip(jnp.exp(jax.random.uniform(streams_of[4], (HLAT,), jnp.float32, math.log(0.5), math.log(2.0))), 0.5, 2.0)
    return {"coeffs": coeffs, "legendre": legendre, "pair_first": pair_first, "row_counts": row_counts, "quad_weights": quad_weights}


def member_masks(leading, degrees, waves):
    entry = jnp.arange(degrees, dtype=jnp.int32)[None, :]
    border = (waves - leading)[:, None]
    member_one = (entry < border).astype(jnp.float32)
    member_two = ((entry >= border) & (entry <= waves)).astype(jnp.float32)
    sign_one = (1 - 2 * (entry % 2)).astype(jnp.float32) + 0.0 * member_one
    sign_two = (1 - 2 * ((entry + leading[:, None]) % 2)).astype(jnp.float32)
    return (member_one, member_two, sign_one, sign_two)

def wave_table(waves_col, n_lon, length):
    column = jnp.arange(length, dtype=jnp.int32)
    turns = waves_col[:, None] * column[None, :] % n_lon
    angle = turns.astype(jnp.float32) * (2.0 * math.pi / n_lon)
    scale = 1.0 / math.sqrt(n_lon)
    live = (column < n_lon)[None, :]
    cosine = jnp.where(live, jnp.cos(angle) * scale, 0.0)
    sine = jnp.where(live, -jnp.sin(angle) * scale, 0.0)
    return jnp.stack([cosine, sine]).astype(jnp.bfloat16)

def reference(coeffs, legendre, pair_first, row_counts, quad_weights):
    pieces = 16
    per_piece = PAIRS // pieces
    coeff_blocks = coeffs.reshape(KIN, 2, pieces, per_piece, PAIRLEN).transpose(2, 0, 1, 3, 4)
    table_blocks = legendre.reshape(pieces, per_piece, PAIRLEN, HLAT)
    first_blocks = pair_first.reshape(pieces, per_piece)

    def inverse(operands):
        block, leg_block, leading = operands
        member_one, member_two, sign_one, sign_two = member_masks(leading, PAIRLEN, WAVES)
        selector = jnp.stack([member_one, member_one * sign_one, member_two, member_two * sign_two])
        spread = block.astype(jnp.float32)[None] * selector[:, None, None]
        products = jnp.einsum('qkrpt,ptl->qkrpl', spread, leg_block.astype(jnp.float32))
        north = jnp.stack([products[0], products[2]], axis=3)
        south = jnp.stack([products[1], products[3]], axis=3)
        return jnp.concatenate([north, south[..., ::-1]], axis=-1).astype(jnp.bfloat16)
    fourier_parts = lax.map(inverse, (coeff_blocks, table_blocks, first_blocks))
    fourier_rows = fourier_parts.transpose(1, 2, 0, 3, 4, 5).reshape(KIN, 2, WAVES, NLAT)
    waves_col = jnp.stack([pair_first, WAVES - 1 - pair_first], axis=1).reshape(WAVES)
    table = wave_table(waves_col, NLON, NLON).astype(jnp.float32)
    wave_limit = jnp.minimum(WAVES - 1, row_counts // 2 - 1)
    keep_mask = (waves_col[:, None] <= wave_limit[None, :]).astype(jnp.float32)
    factor = jnp.where(waves_col == 0, 1.0, 2.0).astype(jnp.float32)[:, None]
    latitude = jnp.arange(NLAT, dtype=jnp.int32)
    weight_rows = quad_weights[jnp.minimum(latitude, NLAT - 1 - latitude)]
    lat_block = NLAT // pieces
    fourier_blocks = fourier_rows.reshape(KIN, 2, WAVES, pieces, lat_block).transpose(3, 0, 1, 2, 4)
    keep_blocks = keep_mask.reshape(WAVES, pieces, lat_block).transpose(1, 0, 2)
    weight_blocks = weight_rows.reshape(pieces, lat_block)

    def grid_step(operands):
        block, keep_here, weight_here = operands
        scaled = block.astype(jnp.float32) * (keep_here * factor)[None, None]
        grid_fields = jnp.einsum('krml,rmj->klj', scaled, table)
        fields = grid_fields.reshape(LEVELS, 3, lat_block, NLON)
        grid_flux = jnp.stack([fields[:, 0] * fields[:, 2], fields[:, 1] * fields[:, 2]], axis=1)
        grid_flux = grid_flux.reshape(KOUT, lat_block, NLON).astype(jnp.bfloat16)
        spectra = jnp.einsum('klj,rmj->krml', grid_flux.astype(jnp.float32), table)
        return (spectra * (keep_here * weight_here[None, :])[None, None]).astype(jnp.bfloat16)
    spectra_parts = lax.map(grid_step, (fourier_blocks, keep_blocks, weight_blocks))
    weighted_spectra = spectra_parts.transpose(1, 2, 3, 0, 4).reshape(KOUT, 2, WAVES, NLAT)
    spectra_blocks = weighted_spectra.reshape(KOUT, 2, pieces, per_piece, 2, NLAT).transpose(2, 0, 1, 3, 4, 5)

    def direct(operands):
        block, leg_block, leading = operands
        values = block.astype(jnp.float32)
        north = values[..., :HLAT]
        south = values[..., HLAT:][..., ::-1]
        leg_float = leg_block.astype(jnp.float32)
        north_sum = jnp.einsum('krpel,ptl->ekrpt', north, leg_float)
        south_sum = jnp.einsum('krpel,ptl->ekrpt', south, leg_float)
        member_one, member_two, sign_one, sign_two = member_masks(leading, PAIRLEN, WAVES)
        return member_one * (north_sum[0] + sign_one * south_sum[0]) + member_two * (north_sum[1] + sign_two * south_sum[1])
    result_parts = lax.map(direct, (spectra_blocks, table_blocks, first_blocks))
    return result_parts.transpose(1, 2, 0, 3, 4).reshape(KOUT, 2, PAIRS, PAIRLEN).astype(jnp.bfloat16)
```

```python
import functools

import jax
import jax.numpy as jnp
import ml_dtypes
import numpy as np
from jax import lax
from jax.experimental import pallas as pl
from jax.experimental.pallas import tpu as pltpu
from jax.sharding import PartitionSpec as P

MESH = pl.DeviceIdType.MESH
F32 = jnp.float32
BF16 = jnp.bfloat16
WAVES = 1024
NLON = 5136
QUARTER = NLON // 4
JPAD = 1408
HALF = WAVES // 2
PAIRLEN = 1152
HLAT = 1280
LATS = 32
LEVS = 8
RLEN = HLAT // LATS
LANES = 128
LTILES = HLAT // LANES
KIN = 24
DEVICES = LATS * LEVS
JTILES = ((0, 256), (256, 256), (512, 256), (768, 256), (1024, 256), (1280, 128))


def table_constant():
    column = np.arange(JPAD, dtype=np.int64)[None, :]
    row = np.arange(HALF, dtype=np.int64)[:, None]
    live = column <= QUARTER
    scale = 1.0 / np.sqrt(NLON)
    parts = []
    for fn in (np.cos, lambda x: -np.sin(x)):
        for wave in (2 * row, WAVES - 1 - 2 * row):
            angle = (wave * column % NLON) * (2.0 * np.pi / NLON)
            parts.append(np.where(live, fn(angle) * scale, 0.0))
    return np.concatenate(parts, axis=1).astype(np.float32).astype(ml_dtypes.bfloat16)


def coords():
    a, b = lax.axis_index("lat"), lax.axis_index("lev")
    return a // 4, a % 4, b // 2, b % 2


def lat_peer(i):
    z, x, _, _ = coords()
    return ((z + i % 8) % 8) * 4 + (x + i // 8) % 4


def lev_peer(i):
    _, _, y, c = coords()
    return ((y + i // 2) % 4) * 2 + (c + i % 2) % 2


def lane_iota(rows):
    return lax.broadcasted_iota(jnp.int32, (rows, LANES), 1)


def left(x, by):
    by = by % LANES
    return x if by == 0 else pltpu.roll(x, LANES - by, 1)


def kernel(
    coeffs, leg_hbm, tab_hbm, first_smem, first_row, limits, quad, out,
    leg, tab0, tab, ys, send, recv, xs, xt, flux, send_back, recv_back, dsp, rs, mw,
    leg_sem, tab_sem, own_sem, send_sem, recv_sem, back_send_sem, back_recv_sem, ready_sem,
):
    a_me, b_me = lax.axis_index("lat"), lax.axis_index("lev")
    me = a_me * LEVS + b_me

    barrier = pltpu.get_barrier_semaphore()

    def greet_lev(i, carry):
        pl.semaphore_signal(barrier, inc=1, device_id=(a_me, lev_peer(i)), device_id_type=MESH)
        return carry

    def greet_lat(i, carry):
        pl.semaphore_signal(barrier, inc=1, device_id=(lat_peer(i), b_me), device_id_type=MESH)
        return carry

    leg_copies = [pltpu.make_async_copy(leg_hbm.at[p], leg.at[p], leg_sem.at[p]) for p in range(2)]
    tab_copy = pltpu.make_async_copy(tab_hbm, tab0, tab_sem)
    for copy in leg_copies:
        copy.start()
    tab_copy.start()
    lax.fori_loop(1, LEVS, greet_lev, 0)
    lax.fori_loop(1, LATS, greet_lat, 0)

    entry = lax.broadcasted_iota(jnp.int32, (1, PAIRLEN), 1)
    alternating = (1 - 2 * (entry % 2)).astype(F32)
    masks, signs = [], []
    for p in range(2):
        first = first_smem[2 * me + p]
        border = WAVES - first
        is_odd = first % 2
        one = (entry < border).astype(F32)
        two = ((entry >= border) & (entry <= WAVES)).astype(F32)
        odd = is_odd.astype(F32)
        masks.append((one + odd * (two - one), two + odd * (one - two)))
        signs.append((alternating * (1.0 - 2.0 * odd), alternating))
        even_wave = first + is_odd * (WAVES - 1 - 2 * first)
        waves = (even_wave, WAVES - 1 - even_wave)
        factors = [jnp.where(w == 0, 1.0, 2.0) for w in waves]
        kept = [[(limits[s : s + 1, :] >= w).astype(F32) for w in waves] for s in range(2)]
        rows = []
        for side in range(2):
            for c in range(2):
                values = coeffs[p, c].astype(F32)
                for par in range(2):
                    chosen = masks[p][par] * signs[p][par] if side else masks[p][par]
                    rows.append(values * chosen)
                    mw[p * 8 + side * 4 + c * 2 + par : p * 8 + side * 4 + c * 2 + par + 1, :] = (
                        kept[side][par] * quad[...]
                    )
        spread = jnp.concatenate(rows, axis=0).astype(BF16)
        leg_copies[p].wait()
        for lt in range(0, LTILES, 2):
            at = lt * LANES
            product = jnp.dot(spread, leg[p, :, at : at + 2 * LANES], preferred_element_type=F32)
            for side in range(2):
                for par in range(2):
                    scale = kept[side][par][:, at : at + 2 * LANES] * factors[par]
                    for c in range(2):
                        kind = side * 4 + c * 2 + par
                        piece = product[kind * KIN : (kind + 1) * KIN] * scale
                        for half in range(2):
                            ys[lt + half, p * 192 + kind * KIN : p * 192 + (kind + 1) * KIN, :] = piece[
                                :, half * LANES : (half + 1) * LANES
                            ]

    pl.semaphore_wait(barrier, LEVS - 1 + LATS - 1)

    def greet_ready(i, carry):
        pl.semaphore_signal(ready_sem, inc=1, device_id=(lat_peer(i), b_me), device_id_type=MESH)
        return carry

    lax.fori_loop(1, LATS, greet_ready, 0)

    lane16 = lane_iota(16)

    def make_and_send(i, carry):
        b = lev_peer(i)
        fields = [
            [ys[lt, pl.ds(3 * b + f, 16, stride=KIN), :] for lt in range(LTILES)] for f in range(3)
        ]
        for a in range(LATS):
            tile, shift = divmod(a * RLEN, LANES)
            parts = []
            for f in range(3):
                part = fields[f][tile]
                if shift + RLEN > LANES:
                    part = jnp.where(lane16 >= shift, part, fields[f][tile + 1])
                parts.append(left(part, shift - f * RLEN))
            block = jnp.where(lane16 < RLEN, parts[0], jnp.where(lane16 < 2 * RLEN, parts[1], parts[2]))
            send[a, b] = block.astype(BF16)

        @pl.when(i == 0)
        def _():
            pl.semaphore_wait(ready_sem, LATS - 1)

        def go(l, carry):
            a = lat_peer(l)
            pltpu.make_async_remote_copy(
                src_ref=send.at[a, b],
                dst_ref=recv.at[me],
                send_sem=send_sem,
                recv_sem=recv_sem,
                device_id=(a, b),
                device_id_type=MESH,
            ).start()
            return carry

        lax.fori_loop(jnp.where(i == 0, 1, 0), LATS, go, 0)
        return carry

    lax.fori_loop(0, LEVS, make_and_send, 0)
    own = pltpu.make_async_copy(send.at[a_me, b_me], recv.at[me], own_sem)
    own.start()

    tab_copy.wait()
    firsts = first_row[...]
    slot_row = jnp.where(firsts % 2 == 0, firsts, WAVES - 1 - firsts) // 2
    chosen = (lax.broadcasted_iota(jnp.int32, (HALF, HALF), 0) == slot_row).astype(F32)
    pick = jnp.transpose(chosen).astype(BF16)

    def permute(n, carry):
        at = pl.ds(pl.multiple_of(n * 256, 256), 256)
        tab[:, at] = jnp.dot(pick, tab0[:, at], preferred_element_type=F32).astype(BF16)
        return carry

    lax.fori_loop(0, 4 * JPAD // 256, permute, 0)

    own.wait()
    others = pl.ds(0, DEVICES - 1)
    pltpu.make_async_copy(recv.at[others], recv.at[others], recv_sem).wait()

    def unpack(n, carry):
        blocks = recv[pl.ds(n * 16, 16)].astype(F32).reshape(256, LANES)
        xs[pl.ds(pl.multiple_of(n * 256, 256), 256), :] = blocks
        return carry

    lax.fori_loop(0, DEVICES // 16, unpack, 0)
    for side in range(2):
        for cp in range(4):
            for q in range(4):
                block = xs[pl.ds(q * 1024 + side * 4 + cp, LANES, stride=8), :]
                xt[cp, side * LANES : (side + 1) * LANES, q * LANES : (q + 1) * LANES] = jnp.transpose(
                    block
                ).astype(BF16)

    for cp in range(4):
        for side in range(2):
            flux[cp, side * LANES + 2 * RLEN : (side + 1) * LANES, :] = jnp.zeros((LANES - 2 * RLEN, JPAD), BF16)
    for at, width in JTILES:
        ce, co, se, so = (
            jnp.dot(xt[cp], tab[:, cp * JPAD + at : cp * JPAD + at + width], preferred_element_type=F32)
            for cp in range(4)
        )
        column = at + lax.broadcasted_iota(jnp.int32, (1, width), 1)
        half = jnp.where((column == 0) | (column == QUARTER), 0.5, 1.0)
        plus, minus, sums, diffs = ce + co, ce - co, se + so, se - so
        grids = (plus + sums, plus - sums, minus - diffs, minus + diffs)
        for side in range(2):
            base = side * LANES
            fl = []
            for g in grids:
                q = g[base + 2 * RLEN : base + 3 * RLEN] * half
                fl.append(g[base : base + 2 * RLEN] * jnp.concatenate([q, q], axis=0))
            s12, d12, s34, d34 = fl[0] + fl[1], fl[0] - fl[1], fl[2] + fl[3], fl[3] - fl[2]
            for cp, value in enumerate((s12 + s34, s12 - s34, d12 + d34, d12 - d34)):
                flux[cp, base : base + 2 * RLEN, at : at + width] = value.astype(BF16)

    for cp in range(4):
        spectra = lax.dot_general(
            tab[:, cp * JPAD : (cp + 1) * JPAD], flux[cp], (((1,), (1,)), ((), ())), preferred_element_type=F32
        )
        for side in range(2):
            xs[pl.ds(side * 4 + cp, HALF, stride=8), :] = spectra[:, side * LANES : (side + 1) * LANES]

    def pack(n, carry):
        rows = xs[pl.ds(pl.multiple_of(n * 256, 256), 256), :]
        send_back[pl.ds(n * 16, 16)] = rows.reshape(16, 16, LANES).astype(BF16)
        return carry

    lax.fori_loop(0, DEVICES // 16, pack, 0)

    def go_back(i, carry):
        a, b = lat_peer(i % LATS), lev_peer(i // LATS)
        pltpu.make_async_remote_copy(
            src_ref=send_back.at[a * LEVS + b],
            dst_ref=recv_back.at[me],
            send_sem=back_send_sem,
            recv_sem=back_recv_sem,
            device_id=(a, b),
            device_id_type=MESH,
        ).start()
        return carry

    lax.fori_loop(1, DEVICES, go_back, 0)
    own = pltpu.make_async_copy(send_back.at[me], recv_back.at[me], own_sem)
    own.start()
    own.wait()
    pltpu.make_async_copy(recv_back.at[others], recv_back.at[others], back_recv_sem).wait()

    def gather(b, carry):
        blocks = [recv_back[a * LEVS + b].astype(F32) for a in range(LATS)]
        for lt in range(LTILES):
            comps = []
            for comp in range(2):
                whole = None
                for a in range(lt * LANES // RLEN, (lt * LANES + LANES - 1) // RLEN + 1):
                    start = a * RLEN - lt * LANES
                    part = left(blocks[a], comp * RLEN - start)
                    whole = part if whole is None else jnp.where(lane16 >= start, part, whole)
                comps.append(whole * mw[:, lt * LANES : (lt + 1) * LANES])
            for p in range(2):
                both = jnp.concatenate([comps[0][p * 8 : p * 8 + 8], comps[1][p * 8 : p * 8 + 8]], axis=0)
                dsp[p, pl.ds(pl.multiple_of(b * 16, 16), 16), lt * LANES : (lt + 1) * LANES] = both.astype(BF16)
        return carry

    lax.fori_loop(0, LEVS, gather, 0)

    for p in range(2):
        for n in range(PAIRLEN // LANES):
            rs[n] = lax.dot_general(
                dsp[p], leg[p, n * LANES : (n + 1) * LANES, :], (((1,), (1,)), ((), ())), preferred_element_type=F32
            )
            at = slice(n * LANES, (n + 1) * LANES)
            for c in range(2):
                total = None
                for par in range(2):
                    north = rs[n, pl.ds(c * 2 + par, 16, stride=8), :]
                    south = rs[n, pl.ds(4 + c * 2 + par, 16, stride=8), :]
                    term = masks[p][par][:, at] * (north + signs[p][par][:, at] * south)
                    total = term if total is None else total + term
                out[p, c, :, at] = total.astype(BF16)

    pltpu.make_async_copy(recv.at[others], recv.at[others], send_sem).wait()
    pltpu.make_async_copy(recv_back.at[others], recv_back.at[others], back_send_sem).wait()


def on_device(table, coeffs, legendre, pair_first, row_counts, quad_weights):
    swapped = coeffs.transpose(2, 1, 0, 3)
    counts = jnp.stack([row_counts[:HLAT], row_counts[HLAT:][::-1]])
    limits = jnp.minimum(WAVES - 1, counts // 2 - 1)
    vmem = pl.BlockSpec(memory_space=pltpu.VMEM)
    any_space = pl.BlockSpec(memory_space=pl.ANY)
    result = pl.pallas_call(
        kernel,
        out_shape=jax.ShapeDtypeStruct((2, 2, 16, PAIRLEN), BF16),
        in_specs=[vmem, any_space, any_space, pl.BlockSpec(memory_space=pltpu.SMEM), vmem, vmem, vmem],
        out_specs=vmem,
        scratch_shapes=[
            pltpu.VMEM((2, PAIRLEN, HLAT), BF16),
            pltpu.VMEM((HALF, 4 * JPAD), BF16),
            pltpu.VMEM((HALF, 4 * JPAD), BF16),
            pltpu.VMEM((LTILES, 384, LANES), F32),
            pltpu.VMEM((LATS, LEVS, 16, LANES), BF16),
            pltpu.VMEM((DEVICES, 16, LANES), BF16),
            pltpu.VMEM((DEVICES * 16, LANES), F32),
            pltpu.VMEM((4, 256, HALF), BF16),
            pltpu.VMEM((4, 256, JPAD), BF16),
            pltpu.VMEM((DEVICES, 16, LANES), BF16),
            pltpu.VMEM((DEVICES, 16, LANES), BF16),
            pltpu.VMEM((2, 128, HLAT), BF16),
            pltpu.VMEM((PAIRLEN // LANES, 128, LANES), F32),
            pltpu.VMEM((16, HLAT), F32),
            pltpu.SemaphoreType.DMA((2,)),
            pltpu.SemaphoreType.DMA,
            pltpu.SemaphoreType.DMA,
            pltpu.SemaphoreType.DMA,
            pltpu.SemaphoreType.DMA,
            pltpu.SemaphoreType.DMA,
            pltpu.SemaphoreType.DMA,
            pltpu.SemaphoreType.REGULAR,
        ],
        compiler_params=pltpu.CompilerParams(
            collective_id=0, has_side_effects=True, vmem_limit_bytes=52 * 2**20
        ),
        name="transforms",
    )(swapped, legendre, table, pair_first, pair_first.reshape(1, HALF), limits, quad_weights.reshape(1, HLAT))
    return result.transpose(2, 1, 0, 3)


def solution(mesh):
    placed = (P(None, None, ("lat", "lev"), None), P(("lat", "lev"), None, None), P(), P(), P())
    table = table_constant()
    return jax.shard_map(
        functools.partial(on_device, table),
        mesh=mesh,
        in_specs=placed,
        out_specs=P(None, None, ("lat", "lev"), None),
        check_vma=False,
    )
```

```python
import functools

import jax
import jax.numpy as jnp
import ml_dtypes
import numpy as np
from jax import lax
from jax.experimental import pallas as pl
from jax.experimental.pallas import tpu as pltpu
from jax.sharding import PartitionSpec as P

MESH = pl.DeviceIdType.MESH
F32 = jnp.float32
BF16 = jnp.bfloat16
WAVES = 1024
NLON = 5136
QUARTER = NLON // 4
JPAD = 1408
HALF = WAVES // 2
PAIRLEN = 1152
HLAT = 1280
LATS = 32
LEVS = 8
RLEN = HLAT // LATS
LANES = 128
LTILES = HLAT // LANES
KIN = 24
DEVICES = LATS * LEVS
JTILES = ((0, 256), (256, 256), (512, 256), (768, 256), (1024, 256), (1280, 128))


def table_constant():
    column = np.arange(JPAD, dtype=np.int64)[None, :]
    row = np.arange(HALF, dtype=np.int64)[:, None]
    live = column <= QUARTER
    scale = 1.0 / np.sqrt(NLON)
    parts = []
    for fn in (np.cos, lambda x: -np.sin(x)):
        for wave in (2 * row, WAVES - 1 - 2 * row):
            angle = (wave * column % NLON) * (2.0 * np.pi / NLON)
            parts.append(np.where(live, fn(angle) * scale, 0.0))
    return np.concatenate(parts, axis=1).astype(np.float32).astype(ml_dtypes.bfloat16)


def coords():
    a, b = lax.axis_index("lat"), lax.axis_index("lev")
    return a >> 2, a & 3, b >> 1, b & 1


def device(z, x, y, c):
    return ((z & 7) << 2) + (x & 3), ((y & 3) << 1) + (c & 1)


def signal(sem, to):
    pl.semaphore_signal(sem, inc=1, device_id=to, device_id_type=MESH)


def lane_iota(rows):
    return lax.broadcasted_iota(jnp.int32, (rows, LANES), 1)


def left(x, by):
    by = by % LANES
    return x if by == 0 else pltpu.roll(x, LANES - by, 1)


def kernel(
    coeffs_hbm, leg_hbm, tab_hbm, first_hbm, counts_hbm, weights_hbm, out,
    coeffs, first_row, counts, weights, leg, tab0, tab, ys, send, recv, xs, xt, flux, send_lev, mid, send_lat, last, dt, dsp, rs, mw,
    leg_sem, tab_sem, own_sem, send_sem, recv_sem, lev_send_sem, lev_recv_sem, lat_send_sem, lat_recv_sem,
    round_sem, small_sem,
):
    a_me, b_me = lax.axis_index("lat"), lax.axis_index("lev")
    me = a_me * LEVS + b_me
    z_me, x_me, y_me, c_me = coords()

    half_lanes = HLAT // 2
    leg_copies = [
        [
            pltpu.make_async_copy(
                leg_hbm.at[p, :, pl.ds(h * half_lanes, half_lanes)],
                leg.at[p, :, pl.ds(h * half_lanes, half_lanes)],
                leg_sem.at[2 * h + p],
            )
            for p in range(2)
        ]
        for h in range(2)
    ]
    tab_copy = pltpu.make_async_copy(tab_hbm, tab0, tab_sem)
    small_copies = [
        pltpu.make_async_copy(src, dst, small_sem.at[n])
        for n, (src, dst) in enumerate(
            ((first_hbm, first_row), (counts_hbm, counts), (weights_hbm, weights), (coeffs_hbm, coeffs))
        )
    ]
    for copy in small_copies + leg_copies[0] + leg_copies[1]:
        copy.start()

    barrier = pltpu.get_barrier_semaphore()
    x_line = [device(z_me, x_me + i, y_me, c_me) for i in range(1, 4)]
    lev_group = [device(z_me, x_me, y_me + i // 2, c_me + i % 2) for i in range(1, LEVS)]
    for to in [device(z_me + i, x_me, y_me, c_me) for i in range(1, 8)] + x_line + lev_group:
        signal(barrier, to)

    for copy in small_copies:
        copy.wait()
    firsts = first_row[...].reshape(1, HALF)
    slots = lax.broadcasted_iota(jnp.int32, (1, HALF), 1)
    entry = lax.broadcasted_iota(jnp.int32, (1, PAIRLEN), 1)
    alternating = (1 - 2 * (entry % 2)).astype(F32)
    masks, signs, spreads, scales = [], [], [], []
    quad = weights[...].reshape(1, HLAT)
    limits = jnp.minimum(WAVES - 1, counts[...].reshape(1, 2 * HLAT) // 2 - 1)
    flip = (
        lax.broadcasted_iota(jnp.int32, (LANES, LANES), 0) + lax.broadcasted_iota(jnp.int32, (LANES, LANES), 1)
        == LANES - 1
    ).astype(BF16)
    tiles = jnp.concatenate(
        [limits[:, (2 * LTILES - 1 - t) * LANES : (2 * LTILES - t) * LANES] for t in range(LTILES)]
        + [jnp.zeros((16 - LTILES, LANES), jnp.int32)],
        axis=0,
    )
    high, low = tiles // 32, tiles % 32
    mirrored = 32.0 * jnp.dot(high.astype(F32).astype(BF16), flip, preferred_element_type=F32) + jnp.dot(
        low.astype(F32).astype(BF16), flip, preferred_element_type=F32
    )
    south = jnp.concatenate([mirrored[t : t + 1, :] for t in range(LTILES)], axis=1)
    sides = (limits[:, :HLAT].astype(F32), south)
    for p in range(2):
        first = jnp.sum(jnp.where(slots == 2 * me + p, firsts, 0), axis=1, keepdims=True)
        border = WAVES - first
        is_odd = first % 2
        one = (entry < border).astype(F32)
        two = ((entry >= border) & (entry <= WAVES)).astype(F32)
        odd = is_odd.astype(F32)
        masks.append((one + odd * (two - one), two + odd * (one - two)))
        signs.append((alternating * (1.0 - 2.0 * odd), alternating))
        even_wave = first + is_odd * (WAVES - 1 - 2 * first)
        waves = [w.astype(F32) for w in (even_wave, WAVES - 1 - even_wave)]
        kept = [[(sides[s] >= w).astype(F32) for w in waves] for s in range(2)]
        scales.append([[kept[s][par] * jnp.where(waves[par] == 0, 1.0, 2.0) for par in range(2)] for s in range(2)])
        rows = []
        for side in range(2):
            for c in range(2):
                values = coeffs[p, c].astype(F32)
                for par in range(2):
                    rows.append(values * (masks[p][par] * signs[p][par] if side else masks[p][par]))
                    kind = p * 8 + side * 4 + c * 2 + par
                    mw[kind : kind + 1, :] = kept[side][par] * quad
        spreads.append(jnp.concatenate(rows, axis=0).astype(BF16))

    def inverse(h, p):
        leg_copies[h][p].wait()
        for lt, count in ((0, 2), (2, 2), (4, 1)):
            at = slice(h * half_lanes + lt * LANES, h * half_lanes + (lt + count) * LANES)
            product = jnp.dot(spreads[p], leg[p, :, at], preferred_element_type=F32)
            for side in range(2):
                for par in range(2):
                    scale = scales[p][side][par][:, at]
                    for c in range(2):
                        kind = side * 4 + c * 2 + par
                        piece = product[kind * KIN : (kind + 1) * KIN] * scale
                        for n in range(count):
                            ys[h * 5 + lt + n, p * 192 + kind * KIN : p * 192 + (kind + 1) * KIN, :] = piece[
                                :, n * LANES : (n + 1) * LANES
                            ]

    lane16 = lane_iota(16)

    def make_and_send(h, core):
        def step(i, carry):
            b = (((y_me + i) & 3) << 1) + core
            fields = [
                [ys[h * 5 + lt, pl.ds(3 * b + f, 16, stride=KIN), :] for lt in range(5)] for f in range(3)
            ]
            for n in range(16):
                tile, shift = divmod(n * RLEN, LANES)
                parts = []
                for f in range(3):
                    part = fields[f][tile]
                    if shift + RLEN > LANES:
                        part = jnp.where(lane16 >= shift, part, fields[f][tile + 1])
                    parts.append(left(part, shift - f * RLEN))
                block = jnp.where(lane16 < RLEN, parts[0], jnp.where(lane16 < 2 * RLEN, parts[1], parts[2]))
                send[h * 16 + n, b] = block.astype(BF16)

            def go(l, carry):
                z, x = (z_me + l) & 7, 2 * h + (((l >> 3) + x_me) & 1)
                a = (z << 2) + x

                @pl.when((b != b_me) | (a != a_me))
                def _():
                    pltpu.make_async_remote_copy(
                        src_ref=send.at[(x << 3) + z, b],
                        dst_ref=recv.at[me],
                        send_sem=send_sem,
                        recv_sem=recv_sem,
                        device_id=(a, b),
                        device_id_type=MESH,
                    ).start()

                return carry

            lax.fori_loop(0, 16, go, 0)
            return carry

        lax.fori_loop(0, 4, step, 0)

    pl.semaphore_wait(barrier, 17)
    for to in x_line:
        signal(round_sem.at[0], to)
    inverse(0, 0)
    pl.semaphore_wait(round_sem.at[0], 3)
    for to in lev_group:
        signal(round_sem.at[1], to)
    inverse(0, 1)
    tab_copy.start()
    pl.semaphore_wait(round_sem.at[1], LEVS - 1)
    make_and_send(0, 0)
    for p in range(2):
        inverse(1, p)
    make_and_send(1, 0)
    make_and_send(0, 1)
    make_and_send(1, 1)
    own = pltpu.make_async_copy(send.at[(x_me << 3) + z_me, b_me], recv.at[me], own_sem)
    own.start()

    tab_copy.wait()
    slot_row = jnp.where(firsts % 2 == 0, firsts, WAVES - 1 - firsts) // 2
    chosen = (lax.broadcasted_iota(jnp.int32, (HALF, HALF), 0) == slot_row).astype(F32)
    pick = jnp.transpose(chosen).astype(BF16)

    def permute(n, carry):
        at = pl.ds(pl.multiple_of(n * 256, 256), 256)
        tab[:, at] = jnp.dot(pick, tab0[:, at], preferred_element_type=F32).astype(BF16)
        return carry

    lax.fori_loop(0, 4 * JPAD // 256, permute, 0)

    own.wait()
    others = pl.ds(0, DEVICES - 1)
    away = ((3, 5), (4, 0), (2, 6), (1, 7))

    def middle():
        pltpu.make_async_copy(recv.at[others], recv.at[others], recv_sem).wait()

        def unpack(n, carry):
            blocks = recv[pl.ds(n * 16, 16)].astype(F32).reshape(256, LANES)
            xs[pl.ds(pl.multiple_of(n * 256, 256), 256), :] = blocks
            return carry

        lax.fori_loop(0, DEVICES // 16, unpack, 0)
        for side in range(2):
            for cp in range(4):
                for q in range(4):
                    block = xs[pl.ds(q * 1024 + side * 4 + cp, LANES, stride=8), :]
                    xt[cp, side * LANES : (side + 1) * LANES, q * LANES : (q + 1) * LANES] = jnp.transpose(
                        block
                    ).astype(BF16)

        for cp in range(4):
            for side in range(2):
                flux[cp, side * LANES + 2 * RLEN : (side + 1) * LANES, :] = jnp.zeros((LANES - 2 * RLEN, JPAD), BF16)
        for at, width in JTILES:
            ce, co, se, so = (
                jnp.dot(xt[cp], tab[:, cp * JPAD + at : cp * JPAD + at + width], preferred_element_type=F32)
                for cp in range(4)
            )
            column = at + lax.broadcasted_iota(jnp.int32, (1, width), 1)
            half = jnp.where((column == 0) | (column == QUARTER), 0.5, 1.0)
            plus, minus, sums, diffs = ce + co, ce - co, se + so, se - so
            grids = (plus + sums, plus - sums, minus - diffs, minus + diffs)
            for side in range(2):
                base = side * LANES
                fl = []
                for g in grids:
                    q = g[base + 2 * RLEN : base + 3 * RLEN] * half
                    fl.append(g[base : base + 2 * RLEN] * jnp.concatenate([q, q], axis=0))
                s12, d12, s34, d34 = fl[0] + fl[1], fl[0] - fl[1], fl[2] + fl[3], fl[3] - fl[2]
                for cp, value in enumerate((s12 + s34, s12 - s34, d12 + d34, d12 - d34)):
                    flux[cp, base : base + 2 * RLEN, at : at + width] = value.astype(BF16)

        for cp in range(4):
            spectra = lax.dot_general(
                tab[:, cp * JPAD : (cp + 1) * JPAD], flux[cp], (((1,), (1,)), ((), ())), preferred_element_type=F32
            )
            for side in range(2):
                xs[pl.ds(side * 4 + cp, HALF, stride=8), :] = spectra[:, side * LANES : (side + 1) * LANES]

    def pack(core, part):
        z = [(z_me + dz) & 7 for dz in away[part]]

        def step(i, carry):
            b = ((((i >> 1) + y_me) & 3) << 1) + ((i + c_me) & 1)
            rows = [
                xs[pl.ds(pl.multiple_of(((((z[n // 4] << 2) + n % 4) << 3) + b) * 16, 16), 16), :] for n in range(8)
            ]
            turned = jnp.transpose(jnp.concatenate(rows, axis=0))
            send_lev[part, b] = turned[: 2 * RLEN].astype(BF16)

            @pl.when(i > 0)
            def _():
                pltpu.make_async_remote_copy(
                    src_ref=send_lev.at[part, b],
                    dst_ref=mid.at[core, part, y_me],
                    send_sem=lev_send_sem,
                    recv_sem=lev_recv_sem.at[core, part],
                    device_id=(a_me, b),
                    device_id_type=MESH,
                ).start()

            return carry

        lax.fori_loop(0, LEVS, step, 0)
        mid[core, part, y_me] = send_lev[part, b_me]

    lane40 = lane_iota(RLEN) // 16
    no_rows = jnp.zeros((8, LANES), F32)

    def relay(core, part):
        for present in (3, 4):

            @pl.when(c_me == (core if present == 3 else 1 - core))
            def _():
                arrived = mid.at[core, part, pl.ds(0, present)]
                pltpu.make_async_copy(arrived, arrived, lev_recv_sem.at[core, part]).wait()

        both = [mid[core, part, y].astype(F32) for y in range(4)]
        arrays = [both[y][comp * RLEN : (comp + 1) * RLEN] for comp in range(2) for y in range(4)]
        for bit in (1, 2, 4):
            low = lane40 & bit == 0
            swapped = list(arrays)
            for n in range(8):
                if not n & bit:
                    one, two = arrays[n], arrays[n + bit]
                    swapped[n] = jnp.where(low, one, pltpu.roll(two, bit * 16, 1))
                    swapped[n + bit] = jnp.where(low, pltpu.roll(one, LANES - bit * 16, 1), two)
            arrays = swapped
        pair = away[part]
        for n in range(8):
            z = (z_me + pair[n // 4]) & 7
            send_lat[core, (z << 2) + n % 4] = jnp.concatenate([arrays[n], no_rows], axis=0).astype(BF16)

        def go(l, carry):
            z, x = (z_me + jnp.where(l < 4, pair[0], pair[1])) & 7, (x_me + l) & 3
            a = (z << 2) + x

            @pl.when(a != a_me)
            def _():
                pltpu.make_async_remote_copy(
                    src_ref=send_lat.at[core, a],
                    dst_ref=last.at[core, a_me],
                    send_sem=lat_send_sem,
                    recv_sem=lat_recv_sem.at[core],
                    device_id=(a, b_me),
                    device_id_type=MESH,
                ).start()

            return carry

        lax.fori_loop(0, 8, go, 0)

    for core in range(2):

        @pl.when(c_me == core)
        def _():
            middle()
            for part in range(4):
                pack(core, part)

        for part in range(4):
            relay(core, part)
        last[core, a_me] = send_lat[core, a_me]

    rest = pl.ds(0, LATS - 1)
    for core in range(2):
        arrived = last.at[core, rest]
        pltpu.make_async_copy(arrived, arrived, lat_recv_sem.at[core]).wait()
        for a in range(LATS):
            at = ((a % 4) * 8 + a // 4) * RLEN
            dt[core, at : at + RLEN, :] = last[core, a].astype(F32)[:RLEN]
    for lt in range(LTILES):
        at = slice(lt * LANES, (lt + 1) * LANES)
        turned = [jnp.transpose(dt[core, at, :]) for core in range(2)]
        for p in range(2):
            weight = mw[p * 8 : p * 8 + 8, at]
            dsp[p, :, at] = jnp.concatenate(
                [
                    turned[b % 2][comp * 64 + b // 2 * 16 + p * 8 : comp * 64 + b // 2 * 16 + p * 8 + 8] * weight
                    for b in range(LEVS)
                    for comp in range(2)
                ],
                axis=0,
            ).astype(BF16)
    for p in range(2):
        product = lax.dot_general(leg[p], dsp[p], (((1,), (1,)), ((), ())), preferred_element_type=F32)
        for n in range(PAIRLEN // LANES):
            at = slice(n * LANES, (n + 1) * LANES)
            rs[n] = jnp.transpose(product[at])
            for c in range(2):
                total = None
                for par in range(2):
                    north = rs[n, pl.ds(c * 2 + par, 16, stride=8), :]
                    south = rs[n, pl.ds(4 + c * 2 + par, 16, stride=8), :]
                    term = masks[p][par][:, at] * (north + signs[p][par][:, at] * south)
                    total = term if total is None else total + term
                out[p, c, :, at] = total.astype(BF16)

    sent = send_lev.at[:, pl.ds(0, LEVS - 1)]
    pltpu.make_async_copy(recv.at[others], recv.at[others], send_sem).wait()
    pltpu.make_async_copy(sent, sent, lev_send_sem).wait()
    pltpu.make_async_copy(last.at[:, rest], last.at[:, rest], lat_send_sem).wait()


def on_device(table, coeffs, legendre, pair_first, row_counts, quad_weights):
    swapped = coeffs.transpose(2, 1, 0, 3)
    vmem = pl.BlockSpec(memory_space=pltpu.VMEM)
    hbm = pl.BlockSpec(memory_space=pltpu.HBM)
    result = pl.pallas_call(
        kernel,
        out_shape=jax.ShapeDtypeStruct((2, 2, 16, PAIRLEN), BF16),
        in_specs=[hbm] * 6,
        out_specs=vmem,
        scratch_shapes=[
            pltpu.VMEM((2, 2, KIN, PAIRLEN), BF16),
            pltpu.VMEM((HALF,), jnp.int32),
            pltpu.VMEM((2 * HLAT,), jnp.int32),
            pltpu.VMEM((HLAT,), F32),
            pltpu.VMEM((2, PAIRLEN, HLAT), BF16),
            pltpu.VMEM((HALF, 4 * JPAD), BF16),
            pltpu.VMEM((HALF, 4 * JPAD), BF16),
            pltpu.VMEM((LTILES, 384, LANES), F32),
            pltpu.VMEM((LATS, LEVS, 16, LANES), BF16),
            pltpu.VMEM((DEVICES, 16, LANES), BF16),
            pltpu.VMEM((DEVICES * 16, LANES), F32),
            pltpu.VMEM((4, 256, HALF), BF16),
            pltpu.VMEM((4, 256, JPAD), BF16),
            pltpu.VMEM((4, LEVS, 2 * RLEN, LANES), BF16),
            pltpu.VMEM((2, 4, 4, 2 * RLEN, LANES), BF16),
            pltpu.VMEM((2, LATS, RLEN + 8, LANES), BF16),
            pltpu.VMEM((2, LATS, RLEN + 8, LANES), BF16),
            pltpu.VMEM((2, HLAT, LANES), F32),
            pltpu.VMEM((2, 128, HLAT), BF16),
            pltpu.VMEM((PAIRLEN // LANES, 128, LANES), F32),
            pltpu.VMEM((16, HLAT), F32),
            pltpu.SemaphoreType.DMA((4,)),
            pltpu.SemaphoreType.DMA,
            pltpu.SemaphoreType.DMA,
            pltpu.SemaphoreType.DMA,
            pltpu.SemaphoreType.DMA,
            pltpu.SemaphoreType.DMA,
            pltpu.SemaphoreType.DMA((2, 4)),
            pltpu.SemaphoreType.DMA,
            pltpu.SemaphoreType.DMA((2,)),
            pltpu.SemaphoreType.REGULAR((2,)),
            pltpu.SemaphoreType.DMA((4,)),
        ],
        compiler_params=pltpu.CompilerParams(
            collective_id=0, has_side_effects=True, vmem_limit_bytes=62 * 2**20
        ),
        name="transforms",
    )(swapped, legendre, table, pair_first, row_counts, quad_weights)
    return result.transpose(2, 1, 0, 3)


def solution(mesh):
    placed = (P(None, None, ("lat", "lev"), None), P(("lat", "lev"), None, None), P(), P(), P())
    table = table_constant()
    return jax.shard_map(
        functools.partial(on_device, table),
        mesh=mesh,
        in_specs=placed,
        out_specs=P(None, None, ("lat", "lev"), None),
        check_vma=False,
    )
```

```python
import functools

import jax
import jax.numpy as jnp
import ml_dtypes
import numpy as np
from jax import lax
from jax.experimental import pallas as pl
from jax.experimental.pallas import tpu as pltpu
from jax.sharding import PartitionSpec as P

MESH = pl.DeviceIdType.MESH
F32 = jnp.float32
BF16 = jnp.bfloat16
WAVES = 1024
NLON = 5136
QUARTER = NLON // 4
JPAD = 1408
HALF = WAVES // 2
PAIRLEN = 1152
HLAT = 1280
LATS = 32
LEVS = 8
RLEN = HLAT // LATS
LANES = 128
LTILES = HLAT // LANES
KIN = 24
DEVICES = LATS * LEVS
JTILES = ((0, 256), (256, 256), (512, 256), (768, 256), (1024, 256), (1280, 128))


def table_constant():
    column = np.arange(JPAD, dtype=np.int64)[None, :]
    row = np.arange(HALF, dtype=np.int64)[:, None]
    live = column <= QUARTER
    scale = 1.0 / np.sqrt(NLON)
    parts = []
    for fn in (np.cos, lambda x: -np.sin(x)):
        for wave in (2 * row, WAVES - 1 - 2 * row):
            angle = (wave * column % NLON) * (2.0 * np.pi / NLON)
            parts.append(np.where(live, fn(angle) * scale, 0.0))
    return np.concatenate(parts, axis=1).astype(np.float32).astype(ml_dtypes.bfloat16)


def coords():
    a, b = lax.axis_index("lat"), lax.axis_index("lev")
    return a >> 2, a & 3, b >> 1, b & 1


def device(z, x, y, c):
    return ((z & 7) << 2) + (x & 3), ((y & 3) << 1) + (c & 1)


def signal(sem, to):
    pl.semaphore_signal(sem, inc=1, device_id=to, device_id_type=MESH)


def lane_iota(rows):
    return lax.broadcasted_iota(jnp.int32, (rows, LANES), 1)


def left(x, by):
    by = by % LANES
    return x if by == 0 else pltpu.roll(x, LANES - by, 1)


def kernel(
    coeffs_hbm, leg_hbm, tab_hbm, first_hbm, counts_hbm, weights_hbm, out,
    coeffs, lines, res, first_row, counts, weights, leg, tab0, tab, ys, send, recv, xs, xt, flux, send_lev, mid, send_lat, last, dt, dsp, rs, mw,
    leg_sem, tab_sem, own_sem, send_sem, recv_sem, lev_send_sem, lev_recv_sem, lat_send_sem, lat_recv_sem,
    round_sem, small_sem,
):
    a_me, b_me = lax.axis_index("lat"), lax.axis_index("lev")
    me = a_me * LEVS + b_me
    z_me, x_me, y_me, c_me = coords()

    half_lanes = HLAT // 2
    leg_copies = [
        [
            pltpu.make_async_copy(
                leg_hbm.at[p, :, pl.ds(h * half_lanes, half_lanes)],
                leg.at[p, :, pl.ds(h * half_lanes, half_lanes)],
                leg_sem.at[2 * h + p],
            )
            for p in range(2)
        ]
        for h in range(2)
    ]
    tab_copy = pltpu.make_async_copy(tab_hbm, tab0, tab_sem)
    small_copies = [
        pltpu.make_async_copy(src, dst, small_sem.at[n])
        for n, (src, dst) in enumerate(
            ((first_hbm, first_row), (counts_hbm, counts), (weights_hbm, weights), (coeffs_hbm, coeffs))
        )
    ]
    for copy in small_copies + leg_copies[0] + leg_copies[1]:
        copy.start()

    barrier = pltpu.get_barrier_semaphore()
    x_line = [device(z_me, x_me + i, y_me, c_me) for i in range(1, 4)]
    lev_group = [device(z_me, x_me, y_me + i // 2, c_me + i % 2) for i in range(1, LEVS)]
    for to in [device(z_me + i, x_me, y_me, c_me) for i in range(1, 8)] + x_line + lev_group:
        signal(barrier, to)

    for copy in small_copies:
        copy.wait()
    firsts = first_row[...].reshape(1, HALF)
    slots = lax.broadcasted_iota(jnp.int32, (1, HALF), 1)
    entry = lax.broadcasted_iota(jnp.int32, (1, PAIRLEN), 1)
    alternating = (1 - 2 * (entry % 2)).astype(F32)
    masks, signs, spreads, scales = [], [], [], []
    unrolled = coeffs[...].astype(F32).reshape(4 * KIN, PAIRLEN)
    for n in range(PAIRLEN // LANES):
        lines[n] = unrolled[:, n * LANES : (n + 1) * LANES]
    quad = weights[...].reshape(1, HLAT)
    limits = jnp.minimum(WAVES - 1, counts[...].reshape(1, 2 * HLAT) // 2 - 1)
    flip = (
        lax.broadcasted_iota(jnp.int32, (LANES, LANES), 0) + lax.broadcasted_iota(jnp.int32, (LANES, LANES), 1)
        == LANES - 1
    ).astype(BF16)
    tiles = jnp.concatenate(
        [limits[:, (2 * LTILES - 1 - t) * LANES : (2 * LTILES - t) * LANES] for t in range(LTILES)]
        + [jnp.zeros((16 - LTILES, LANES), jnp.int32)],
        axis=0,
    )
    high, low = tiles // 32, tiles % 32
    mirrored = 32.0 * jnp.dot(high.astype(F32).astype(BF16), flip, preferred_element_type=F32) + jnp.dot(
        low.astype(F32).astype(BF16), flip, preferred_element_type=F32
    )
    south = jnp.concatenate([mirrored[t : t + 1, :] for t in range(LTILES)], axis=1)
    sides = (limits[:, :HLAT].astype(F32), south)
    for p in range(2):
        first = jnp.sum(jnp.where(slots == 2 * me + p, firsts, 0), axis=1, keepdims=True)
        border = WAVES - first
        is_odd = first % 2
        one = (entry < border).astype(F32)
        two = ((entry >= border) & (entry <= WAVES)).astype(F32)
        odd = is_odd.astype(F32)
        masks.append((one + odd * (two - one), two + odd * (one - two)))
        signs.append((alternating * (1.0 - 2.0 * odd), alternating))
        even_wave = first + is_odd * (WAVES - 1 - 2 * first)
        waves = [w.astype(F32) for w in (even_wave, WAVES - 1 - even_wave)]
        kept = [[(sides[s] >= w).astype(F32) for w in waves] for s in range(2)]
        scales.append([[kept[s][par] * jnp.where(waves[par] == 0, 1.0, 2.0) for par in range(2)] for s in range(2)])
        rows = []
        for side in range(2):
            for c in range(2):
                values = jnp.concatenate(
                    [lines[n, pl.ds(2 * c + p, KIN, stride=4), :] for n in range(PAIRLEN // LANES)], axis=1
                )
                for par in range(2):
                    rows.append(values * (masks[p][par] * signs[p][par] if side else masks[p][par]))
                    kind = p * 8 + side * 4 + c * 2 + par
                    mw[kind : kind + 1, :] = kept[side][par] * quad
        spreads.append(jnp.concatenate(rows, axis=0).astype(BF16))

    def inverse(h, p):
        leg_copies[h][p].wait()
        for lt, count in ((0, 2), (2, 2), (4, 1)):
            at = slice(h * half_lanes + lt * LANES, h * half_lanes + (lt + count) * LANES)
            product = jnp.dot(spreads[p], leg[p, :, at], preferred_element_type=F32)
            for side in range(2):
                for par in range(2):
                    scale = scales[p][side][par][:, at]
                    for c in range(2):
                        kind = side * 4 + c * 2 + par
                        piece = product[kind * KIN : (kind + 1) * KIN] * scale
                        for n in range(count):
                            ys[h * 5 + lt + n, p * 192 + kind * KIN : p * 192 + (kind + 1) * KIN, :] = piece[
                                :, n * LANES : (n + 1) * LANES
                            ]

    lane16 = lane_iota(16)

    def make_and_send(h, core, first=0, last=4):
        def step(i, carry):
            b = (((y_me + i) & 3) << 1) + core
            fields = [
                [ys[h * 5 + lt, pl.ds(3 * b + f, 16, stride=KIN), :] for lt in range(5)] for f in range(3)
            ]
            for n in range(16):
                tile, shift = divmod(n * RLEN, LANES)
                parts = []
                for f in range(3):
                    part = fields[f][tile]
                    if shift + RLEN > LANES:
                        part = jnp.where(lane16 >= shift, part, fields[f][tile + 1])
                    parts.append(left(part, shift - f * RLEN))
                block = jnp.where(lane16 < RLEN, parts[0], jnp.where(lane16 < 2 * RLEN, parts[1], parts[2]))
                send[h * 16 + n, b] = block.astype(BF16)

            def go(l, carry):
                z, x = (z_me + l) & 7, 2 * h + (((l >> 3) + x_me) & 1)
                a = (z << 2) + x

                @pl.when((b != b_me) | (a != a_me))
                def _():
                    pltpu.make_async_remote_copy(
                        src_ref=send.at[(x << 3) + z, b],
                        dst_ref=recv.at[me],
                        send_sem=send_sem,
                        recv_sem=recv_sem,
                        device_id=(a, b),
                        device_id_type=MESH,
                    ).start()

                return carry

            lax.fori_loop(0, 16, go, 0)
            return carry

        lax.fori_loop(first, last, step, 0)

    pl.semaphore_wait(barrier, 17)
    for to in x_line:
        signal(round_sem.at[0], to)
    inverse(0, 0)
    pl.semaphore_wait(round_sem.at[0], 3)
    for to in lev_group:
        signal(round_sem.at[1], to)
    inverse(0, 1)
    tab_copy.start()
    pl.semaphore_wait(round_sem.at[1], LEVS - 1)
    make_and_send(0, 0)
    for p in range(2):
        inverse(1, p)
    make_and_send(1, 0)
    tab_copy.wait()
    slot_row = jnp.where(firsts % 2 == 0, firsts, WAVES - 1 - firsts) // 2
    chosen = (lax.broadcasted_iota(jnp.int32, (HALF, HALF), 0) == slot_row).astype(F32)
    pick = jnp.transpose(chosen).astype(BF16)

    def permute(n, carry):
        at = pl.ds(pl.multiple_of(n * 256, 256), 256)
        tab[:, at] = jnp.dot(pick, tab0[:, at], preferred_element_type=F32).astype(BF16)
        return carry

    lax.fori_loop(0, 4 * JPAD // 256, permute, 0)

    make_and_send(0, 1)

    make_and_send(1, 1)

    own = pltpu.make_async_copy(send.at[(x_me << 3) + z_me, b_me], recv.at[me], own_sem)
    own.start()

    own.wait()
    others = pl.ds(0, DEVICES - 1)
    away = ((3, 5), (4, 0), (2, 6), (1, 7))

    pltpu.make_async_copy(recv.at[others], recv.at[others], recv_sem).wait()

    def unpack(n, carry):
        blocks = recv[pl.ds(n * 16, 16)].astype(F32).reshape(256, LANES)
        xs[pl.ds(pl.multiple_of(n * 256, 256), 256), :] = blocks
        return carry

    lax.fori_loop(0, DEVICES // 16, unpack, 0)
    for side in range(2):
        for cp in range(4):
            for q in range(4):
                block = xs[pl.ds(q * 1024 + side * 4 + cp, LANES, stride=8), :]
                xt[cp, side * LANES : (side + 1) * LANES, q * LANES : (q + 1) * LANES] = jnp.transpose(
                    block
                ).astype(BF16)

    for cp in range(4):
        for side in range(2):
            flux[cp, side * LANES + 2 * RLEN : (side + 1) * LANES, :] = jnp.zeros((LANES - 2 * RLEN, JPAD), BF16)
    for at, width in JTILES:
        ce, co, se, so = (
            jnp.dot(xt[cp], tab[:, cp * JPAD + at : cp * JPAD + at + width], preferred_element_type=F32)
            for cp in range(4)
        )
        column = at + lax.broadcasted_iota(jnp.int32, (1, width), 1)
        half = jnp.where((column == 0) | (column == QUARTER), 0.5, 1.0)
        plus, minus, sums, diffs = ce + co, ce - co, se + so, se - so
        grids = (plus + sums, plus - sums, minus - diffs, minus + diffs)
        for side in range(2):
            base = side * LANES
            fl = []
            for g in grids:
                q = g[base + 2 * RLEN : base + 3 * RLEN] * half
                fl.append(g[base : base + 2 * RLEN] * jnp.concatenate([q, q], axis=0))
            s12, d12, s34, d34 = fl[0] + fl[1], fl[0] - fl[1], fl[2] + fl[3], fl[3] - fl[2]
            for cp, value in enumerate((s12 + s34, s12 - s34, d12 + d34, d12 - d34)):
                flux[cp, base : base + 2 * RLEN, at : at + width] = value.astype(BF16)


    for cp in range(4):
        spectra = lax.dot_general(
            tab[:, cp * JPAD : (cp + 1) * JPAD], flux[cp], (((1,), (1,)), ((), ())), preferred_element_type=F32
        )
        for side in range(2):
            xs[pl.ds(side * 4 + cp, HALF, stride=8), :] = spectra[:, side * LANES : (side + 1) * LANES]

    def pack(part):
        z = [(z_me + dz) & 7 for dz in away[part]]

        for i in range(LEVS):
            b = (((y_me + i // 2) & 3) << 1) + i % 2
            rows = [
                xs[pl.ds(pl.multiple_of(((((z[n // 4] << 2) + n % 4) << 3) + b) * 16, 16), 16), :] for n in range(8)
            ]
            turned = jnp.transpose(jnp.concatenate(rows, axis=0))
            send_lev[part, b] = turned[: 2 * RLEN].astype(BF16)

        def go(i, carry):
            y, c = (y_me + (i >> 1)) & 3, i & 1
            pltpu.make_async_remote_copy(
                src_ref=send_lev.at[part, (y << 1) + c],
                dst_ref=mid.at[part, c, y_me],
                send_sem=lev_send_sem,
                recv_sem=lev_recv_sem.at[part],
                device_id=(a_me, (y << 1) + c_me),
                device_id_type=MESH,
            ).start()
            return carry

        lax.fori_loop(2, LEVS, go, 0)
        for c in range(2):
            mid[part, c, y_me] = send_lev[part, (y_me << 1) + c]

    for part in range(4):
        pack(part)


    lane40 = lane_iota(RLEN) // 16
    no_rows = jnp.zeros((8, LANES), F32)
    for part, pair in enumerate(away):
        arrived = mid.at[part, :, pl.ds(0, 3)]
        pltpu.make_async_copy(arrived, arrived, lev_recv_sem.at[part]).wait()
        for c in range(2):
            both = [mid[part, c, y].astype(F32) for y in range(4)]
            arrays = [both[y][comp * RLEN : (comp + 1) * RLEN] for comp in range(2) for y in range(4)]
            for bit in (1, 2, 4):
                low = lane40 & bit == 0
                swapped = list(arrays)
                for n in range(8):
                    if not n & bit:
                        one, two = arrays[n], arrays[n + bit]
                        swapped[n] = jnp.where(low, one, pltpu.roll(two, bit * 16, 1))
                        swapped[n + bit] = jnp.where(low, pltpu.roll(one, LANES - bit * 16, 1), two)
                arrays = swapped
            for n in range(8):
                z = (z_me + pair[n // 4]) & 7
                send_lat[c * LATS + (z << 2) + n % 4] = jnp.concatenate([arrays[n], no_rows], axis=0).astype(BF16)

        def relay(l, carry):
            z, x, c = (z_me + jnp.where(l & 4 == 0, pair[0], pair[1])) & 7, (x_me + l) & 3, (c_me + (l >> 3)) & 1
            a = (z << 2) + x

            @pl.when((a != a_me) | (c != c_me))
            def _():
                pltpu.make_async_remote_copy(
                    src_ref=send_lat.at[(c << 5) + a],
                    dst_ref=last.at[c_me, a_me],
                    send_sem=lat_send_sem,
                    recv_sem=lat_recv_sem.at[c_me],
                    device_id=(a, (y_me << 1) + c),
                    device_id_type=MESH,
                ).start()

            return carry

        lax.fori_loop(0, 16, relay, 0)
    last[c_me, a_me] = send_lat[(c_me << 5) + a_me]

    for core in range(2):
        for count in (LATS - 1, LATS):

            @pl.when(c_me == (core if count < LATS else 1 - core))
            def _():
                arrived = last.at[core, pl.ds(0, count)]
                pltpu.make_async_copy(arrived, arrived, lat_recv_sem.at[core]).wait()

        for a in range(LATS):
            at = ((a % 4) * 8 + a // 4) * RLEN
            dt[core, at : at + RLEN, :] = last[core, a].astype(F32)[:RLEN]
    for lt in range(LTILES):
        at = slice(lt * LANES, (lt + 1) * LANES)
        turned = [jnp.transpose(dt[core, at, :]) for core in range(2)]
        for p in range(2):
            weight = mw[p * 8 : p * 8 + 8, at]
            dsp[p, :, at] = jnp.concatenate(
                [
                    turned[b % 2][comp * 64 + b // 2 * 16 + p * 8 : comp * 64 + b // 2 * 16 + p * 8 + 8] * weight
                    for b in range(LEVS)
                    for comp in range(2)
                ],
                axis=0,
            ).astype(BF16)
    for p in range(2):
        product = lax.dot_general(leg[p], dsp[p], (((1,), (1,)), ((), ())), preferred_element_type=F32)
        for n in range(PAIRLEN // LANES):
            at = slice(n * LANES, (n + 1) * LANES)
            rs[n] = jnp.transpose(product[at])
            for c in range(2):
                total = None
                for par in range(2):
                    north = rs[n, pl.ds(c * 2 + par, 16, stride=8), :]
                    south = rs[n, pl.ds(4 + c * 2 + par, 16, stride=8), :]
                    term = masks[p][par][:, at] * (north + signs[p][par][:, at] * south)
                    total = term if total is None else total + term
                res[n, pl.ds(2 * c + p, 16, stride=4), :] = total

    for n in range(PAIRLEN // LANES):
        out[:, :, :, n * LANES : (n + 1) * LANES] = res[n].astype(BF16).reshape(16, 2, 2, LANES)
    pltpu.make_async_copy(recv.at[others], recv.at[others], send_sem).wait()
    sent = send_lev.at[:, pl.ds(0, 6)]
    pltpu.make_async_copy(sent, sent, lev_send_sem).wait()
    sent = send_lat.at[pl.ds(0, 2 * LATS - 1)]
    pltpu.make_async_copy(sent, sent, lat_send_sem).wait()


def on_device(table, coeffs, legendre, pair_first, row_counts, quad_weights):
    vmem = pl.BlockSpec(memory_space=pltpu.VMEM)
    hbm = pl.BlockSpec(memory_space=pltpu.HBM)
    result = pl.pallas_call(
        kernel,
        out_shape=jax.ShapeDtypeStruct((16, 2, 2, PAIRLEN), BF16),
        in_specs=[hbm] * 6,
        out_specs=vmem,
        scratch_shapes=[
            pltpu.VMEM((KIN, 2, 2, PAIRLEN), BF16),
            pltpu.VMEM((PAIRLEN // LANES, 4 * KIN, LANES), F32),
            pltpu.VMEM((PAIRLEN // LANES, 64, LANES), F32),
            pltpu.VMEM((HALF,), jnp.int32),
            pltpu.VMEM((2 * HLAT,), jnp.int32),
            pltpu.VMEM((HLAT,), F32),
            pltpu.VMEM((2, PAIRLEN, HLAT), BF16),
            pltpu.VMEM((HALF, 4 * JPAD), BF16),
            pltpu.VMEM((HALF, 4 * JPAD), BF16),
            pltpu.VMEM((LTILES, 384, LANES), F32),
            pltpu.VMEM((LATS, LEVS, 16, LANES), BF16),
            pltpu.VMEM((DEVICES, 16, LANES), BF16),
            pltpu.VMEM((DEVICES * 16, LANES), F32),
            pltpu.VMEM((4, 256, HALF), BF16),
            pltpu.VMEM((4, 256, JPAD), BF16),
            pltpu.VMEM((4, LEVS, 2 * RLEN, LANES), BF16),
            pltpu.VMEM((4, 2, 4, 2 * RLEN, LANES), BF16),
            pltpu.VMEM((2 * LATS, RLEN + 8, LANES), BF16),
            pltpu.VMEM((2, LATS, RLEN + 8, LANES), BF16),
            pltpu.VMEM((2, HLAT, LANES), F32),
            pltpu.VMEM((2, 128, HLAT), BF16),
            pltpu.VMEM((PAIRLEN // LANES, 128, LANES), F32),
            pltpu.VMEM((16, HLAT), F32),
            pltpu.SemaphoreType.DMA((4,)),
            pltpu.SemaphoreType.DMA,
            pltpu.SemaphoreType.DMA,
            pltpu.SemaphoreType.DMA,
            pltpu.SemaphoreType.DMA,
            pltpu.SemaphoreType.DMA,
            pltpu.SemaphoreType.DMA((4,)),
            pltpu.SemaphoreType.DMA,
            pltpu.SemaphoreType.DMA((2,)),
            pltpu.SemaphoreType.REGULAR((2,)),
            pltpu.SemaphoreType.DMA((4,)),
        ],
        compiler_params=pltpu.CompilerParams(
            collective_id=0, has_side_effects=True, vmem_limit_bytes=62 * 2**20
        ),
        name="transforms",
    )(coeffs, legendre, table, pair_first, row_counts, quad_weights)
    return result


def solution(mesh):
    placed = (P(None, None, ("lat", "lev"), None), P(("lat", "lev"), None, None), P(), P(), P())
    table = table_constant()
    return jax.shard_map(
        functools.partial(on_device, table),
        mesh=mesh,
        in_specs=placed,
        out_specs=P(None, None, ("lat", "lev"), None),
        check_vma=False,
    )
```

```python
import functools

import jax
import jax.numpy as jnp
import ml_dtypes
import numpy as np
from jax import lax
from jax.experimental import pallas as pl
from jax.experimental.pallas import tpu as pltpu
from jax.sharding import PartitionSpec as P

MESH = pl.DeviceIdType.MESH
F32 = jnp.float32
BF16 = jnp.bfloat16
WAVES = 1024
NLON = 5136
QUARTER = NLON // 4
JPAD = 1408
HALF = WAVES // 2
PAIRLEN = 1152
HLAT = 1280
LATS = 32
LEVS = 8
RLEN = HLAT // LATS
LANES = 128
LTILES = HLAT // LANES
KIN = 24
DEVICES = LATS * LEVS
JTILES = ((0, 256), (256, 256), (512, 256), (768, 256), (1024, 256), (1280, 128))


def table_constant():
    column = np.arange(JPAD, dtype=np.int64)[None, :]
    row = np.arange(HALF, dtype=np.int64)[:, None]
    live = column <= QUARTER
    scale = 1.0 / np.sqrt(NLON)
    parts = []
    for fn in (np.cos, lambda x: -np.sin(x)):
        for wave in (2 * row, WAVES - 1 - 2 * row):
            angle = (wave * column % NLON) * (2.0 * np.pi / NLON)
            parts.append(np.where(live, fn(angle) * scale, 0.0))
    return np.concatenate(parts, axis=1).astype(np.float32).astype(ml_dtypes.bfloat16)


def coords():
    a, b = lax.axis_index("lat"), lax.axis_index("lev")
    return a >> 2, a & 3, b >> 1, b & 1


def device(z, x, y, c):
    return ((z & 7) << 2) + (x & 3), ((y & 3) << 1) + (c & 1)


def signal(sem, to):
    pl.semaphore_signal(sem, inc=1, device_id=to, device_id_type=MESH)


def lane_iota(rows):
    return lax.broadcasted_iota(jnp.int32, (rows, LANES), 1)


def left(x, by):
    by = by % LANES
    return x if by == 0 else pltpu.roll(x, LANES - by, 1)


def kernel(
    coeffs_hbm, leg_hbm, tab_hbm, first_hbm, counts_hbm, weights_hbm, out,
    coeffs, lines, res, first_row, counts, weights, leg, tab0, tab, ys, send, recv, xs, xt, flux, send_lev, mid, send_lat, last, dt, dsp, rs, mw,
    leg_sem, tab_sem, own_sem, send_sem, recv_sem, lev_send_sem, lev_recv_sem, lat_send_sem, lat_recv_sem,
    round_sem, small_sem,
):
    a_me, b_me = lax.axis_index("lat"), lax.axis_index("lev")
    me = a_me * LEVS + b_me
    z_me, x_me, y_me, c_me = coords()

    half_lanes = HLAT // 2
    leg_copies = [
        [
            pltpu.make_async_copy(
                leg_hbm.at[p, :, pl.ds(h * half_lanes, half_lanes)],
                leg.at[p, :, pl.ds(h * half_lanes, half_lanes)],
                leg_sem.at[2 * h + p],
            )
            for p in range(2)
        ]
        for h in range(2)
    ]
    tab_copy = pltpu.make_async_copy(tab_hbm, tab0, tab_sem)
    small_copies = [
        pltpu.make_async_copy(src, dst, small_sem.at[n])
        for n, (src, dst) in enumerate(
            ((first_hbm, first_row), (counts_hbm, counts), (weights_hbm, weights), (coeffs_hbm, coeffs))
        )
    ]
    for copy in small_copies + leg_copies[0] + leg_copies[1]:
        copy.start()

    barrier = pltpu.get_barrier_semaphore()
    x_line = [device(z_me, x_me + i, y_me, c_me) for i in range(1, 4)]
    lev_group = [device(z_me, x_me, y_me + i // 2, c_me + i % 2) for i in range(1, LEVS)]
    for to in [device(z_me + i, x_me, y_me, c_me) for i in range(1, 8)] + x_line + lev_group:
        signal(barrier, to)

    pl.semaphore_wait(barrier, 17)
    for to in x_line:
        signal(round_sem.at[0], to)
    for copy in small_copies:
        copy.wait()
    firsts = first_row[...].reshape(1, HALF)
    slots = lax.broadcasted_iota(jnp.int32, (1, HALF), 1)
    entry = lax.broadcasted_iota(jnp.int32, (1, PAIRLEN), 1)
    alternating = (1 - 2 * (entry % 2)).astype(F32)
    masks, signs, spreads, scales = [], [], [], []
    unrolled = coeffs[...].astype(F32).reshape(4 * KIN, PAIRLEN)
    for n in range(PAIRLEN // LANES):
        lines[n] = unrolled[:, n * LANES : (n + 1) * LANES]
    quad = weights[...].reshape(1, HLAT)
    limits = jnp.minimum(WAVES - 1, counts[...].reshape(1, 2 * HLAT) // 2 - 1)
    flip = (
        lax.broadcasted_iota(jnp.int32, (LANES, LANES), 0) + lax.broadcasted_iota(jnp.int32, (LANES, LANES), 1)
        == LANES - 1
    ).astype(BF16)
    tiles = jnp.concatenate(
        [limits[:, (2 * LTILES - 1 - t) * LANES : (2 * LTILES - t) * LANES] for t in range(LTILES)]
        + [jnp.zeros((16 - LTILES, LANES), jnp.int32)],
        axis=0,
    )
    high, low = tiles // 32, tiles % 32
    mirrored = 32.0 * jnp.dot(high.astype(F32).astype(BF16), flip, preferred_element_type=F32) + jnp.dot(
        low.astype(F32).astype(BF16), flip, preferred_element_type=F32
    )
    south = jnp.concatenate([mirrored[t : t + 1, :] for t in range(LTILES)], axis=1)
    sides = (limits[:, :HLAT].astype(F32), south)
    for p in range(2):
        first = jnp.sum(jnp.where(slots == 2 * me + p, firsts, 0), axis=1, keepdims=True)
        border = WAVES - first
        is_odd = first % 2
        one = (entry < border).astype(F32)
        two = ((entry >= border) & (entry <= WAVES)).astype(F32)
        odd = is_odd.astype(F32)
        masks.append((one + odd * (two - one), two + odd * (one - two)))
        signs.append((alternating * (1.0 - 2.0 * odd), alternating))
        even_wave = first + is_odd * (WAVES - 1 - 2 * first)
        waves = [w.astype(F32) for w in (even_wave, WAVES - 1 - even_wave)]
        kept = [[(sides[s] >= w).astype(F32) for w in waves] for s in range(2)]
        scales.append([[kept[s][par] * jnp.where(waves[par] == 0, 1.0, 2.0) for par in range(2)] for s in range(2)])
        rows = []
        for side in range(2):
            for c in range(2):
                values = jnp.concatenate(
                    [lines[n, pl.ds(2 * c + p, KIN, stride=4), :] for n in range(PAIRLEN // LANES)], axis=1
                )
                for par in range(2):
                    rows.append(values * (masks[p][par] * signs[p][par] if side else masks[p][par]))
                    kind = p * 8 + side * 4 + c * 2 + par
                    mw[kind : kind + 1, :] = kept[side][par] * quad
        spreads.append(jnp.concatenate(rows, axis=0).astype(BF16))

    def inverse(h, p):
        leg_copies[h][p].wait()
        for lt, count in ((0, 2), (2, 2), (4, 1)):
            at = slice(h * half_lanes + lt * LANES, h * half_lanes + (lt + count) * LANES)
            product = jnp.dot(spreads[p], leg[p, :, at], preferred_element_type=F32)
            for side in range(2):
                for par in range(2):
                    scale = scales[p][side][par][:, at]
                    for c in range(2):
                        kind = side * 4 + c * 2 + par
                        piece = product[kind * KIN : (kind + 1) * KIN] * scale
                        for n in range(count):
                            ys[h * 5 + lt + n, p * 192 + kind * KIN : p * 192 + (kind + 1) * KIN, :] = piece[
                                :, n * LANES : (n + 1) * LANES
                            ]

    lane16 = lane_iota(16)

    def make_and_send(h, core, first=0, last=4):
        def step(i, carry):
            b = (((y_me + i) & 3) << 1) + core
            fields = [
                [ys[h * 5 + lt, pl.ds(3 * b + f, 16, stride=KIN), :] for lt in range(5)] for f in range(3)
            ]
            for n in range(16):
                tile, shift = divmod(n * RLEN, LANES)
                parts = []
                for f in range(3):
                    part = fields[f][tile]
                    if shift + RLEN > LANES:
                        part = jnp.where(lane16 >= shift, part, fields[f][tile + 1])
                    parts.append(left(part, shift - f * RLEN))
                block = jnp.where(lane16 < RLEN, parts[0], jnp.where(lane16 < 2 * RLEN, parts[1], parts[2]))
                send[h * 16 + n, b] = block.astype(BF16)

            def go(l, carry):
                z, x = (z_me + l) & 7, 2 * h + (((l >> 3) + x_me) & 1)
                a = (z << 2) + x

                @pl.when((b != b_me) | (a != a_me))
                def _():
                    pltpu.make_async_remote_copy(
                        src_ref=send.at[(x << 3) + z, b],
                        dst_ref=recv.at[me],
                        send_sem=send_sem,
                        recv_sem=recv_sem,
                        device_id=(a, b),
                        device_id_type=MESH,
                    ).start()

                return carry

            lax.fori_loop(0, 16, go, 0)
            return carry

        lax.fori_loop(first, last, step, 0)

    pl.semaphore_wait(round_sem.at[0], 3)
    for to in lev_group:
        signal(round_sem.at[1], to)
    inverse(0, 0)
    inverse(0, 1)
    tab_copy.start()
    pl.semaphore_wait(round_sem.at[1], LEVS - 1)
    make_and_send(0, 0)
    for p in range(2):
        inverse(1, p)
    make_and_send(1, 0)
    make_and_send(0, 1)

    make_and_send(1, 1)

    own = pltpu.make_async_copy(send.at[(x_me << 3) + z_me, b_me], recv.at[me], own_sem)
    own.start()

    tab_copy.wait()
    slot_row = jnp.where(firsts % 2 == 0, firsts, WAVES - 1 - firsts) // 2
    chosen = (lax.broadcasted_iota(jnp.int32, (HALF, HALF), 0) == slot_row).astype(F32)
    pick = jnp.transpose(chosen).astype(BF16)

    def permute(n, carry):
        at = pl.ds(pl.multiple_of(n * 256, 256), 256)
        tab[:, at] = jnp.dot(pick, tab0[:, at], preferred_element_type=F32).astype(BF16)
        return carry

    lax.fori_loop(0, 4 * JPAD // 256, permute, 0)

    for cp in range(4):
        for side in range(2):
            flux[cp, side * LANES + 2 * RLEN : (side + 1) * LANES, :] = jnp.zeros((LANES - 2 * RLEN, JPAD), BF16)
    own.wait()
    others = pl.ds(0, DEVICES - 1)
    away = ((3, 5), (4, 0), (2, 6), (1, 7))

    pltpu.make_async_copy(recv.at[others], recv.at[others], recv_sem).wait()

    def unpack(n, carry):
        blocks = recv[pl.ds(n * 16, 16)].astype(F32).reshape(256, LANES)
        xs[pl.ds(pl.multiple_of(n * 256, 256), 256), :] = blocks
        return carry

    lax.fori_loop(0, DEVICES // 16, unpack, 0, unroll=4)
    for side in range(2):
        for cp in range(4):
            for q in range(4):
                block = xs[pl.ds(q * 1024 + side * 4 + cp, LANES, stride=8), :]
                xt[cp, side * LANES : (side + 1) * LANES, q * LANES : (q + 1) * LANES] = jnp.transpose(
                    block
                ).astype(BF16)

    for at, width in JTILES:
        ce, co, se, so = (
            jnp.dot(xt[cp], tab[:, cp * JPAD + at : cp * JPAD + at + width], preferred_element_type=F32)
            for cp in range(4)
        )
        column = at + lax.broadcasted_iota(jnp.int32, (1, width), 1)
        half = jnp.where((column == 0) | (column == QUARTER), 0.5, 1.0)
        plus, minus, sums, diffs = ce + co, ce - co, se + so, se - so
        grids = (plus + sums, plus - sums, minus - diffs, minus + diffs)
        for side in range(2):
            base = side * LANES
            fl = []
            for g in grids:
                q = g[base + 2 * RLEN : base + 3 * RLEN] * half
                fl.append(g[base : base + 2 * RLEN] * jnp.concatenate([q, q], axis=0))
            s12, d12, s34, d34 = fl[0] + fl[1], fl[0] - fl[1], fl[2] + fl[3], fl[3] - fl[2]
            for cp, value in enumerate((s12 + s34, s12 - s34, d12 + d34, d12 - d34)):
                flux[cp, base : base + 2 * RLEN, at : at + width] = value.astype(BF16)


    for cp in range(4):
        spectra = lax.dot_general(
            tab[:, cp * JPAD : (cp + 1) * JPAD], flux[cp], (((1,), (1,)), ((), ())), preferred_element_type=F32
        )
        for side in range(2):
            xs[pl.ds(side * 4 + cp, HALF, stride=8), :] = spectra[:, side * LANES : (side + 1) * LANES]

    def pack(part):
        z = [(z_me + dz) & 7 for dz in away[part]]

        for i in range(LEVS):
            b = (((y_me + i // 2) & 3) << 1) + i % 2
            rows = [
                xs[pl.ds(pl.multiple_of(((((z[n // 4] << 2) + n % 4) << 3) + b) * 16, 16), 16), :] for n in range(8)
            ]
            turned = jnp.transpose(jnp.concatenate(rows, axis=0))
            send_lev[part, b] = turned[: 2 * RLEN].astype(BF16)

        def go(i, carry):
            y, c = (y_me + (i >> 1)) & 3, i & 1
            pltpu.make_async_remote_copy(
                src_ref=send_lev.at[part, (y << 1) + c],
                dst_ref=mid.at[part, c, y_me],
                send_sem=lev_send_sem,
                recv_sem=lev_recv_sem.at[part],
                device_id=(a_me, (y << 1) + c_me),
                device_id_type=MESH,
            ).start()
            return carry

        lax.fori_loop(2, LEVS, go, 0)
        for c in range(2):
            mid[part, c, y_me] = send_lev[part, (y_me << 1) + c]

    for part in range(4):
        pack(part)


    lane40 = lane_iota(RLEN) // 16
    no_rows = jnp.zeros((8, LANES), F32)
    for part, pair in enumerate(away):
        arrived = mid.at[part, :, pl.ds(0, 3)]
        pltpu.make_async_copy(arrived, arrived, lev_recv_sem.at[part]).wait()
        for c in range(2):
            both = [mid[part, c, y].astype(F32) for y in range(4)]
            arrays = [both[y][comp * RLEN : (comp + 1) * RLEN] for comp in range(2) for y in range(4)]
            for bit in (1, 2, 4):
                low = lane40 & bit == 0
                swapped = list(arrays)
                for n in range(8):
                    if not n & bit:
                        one, two = arrays[n], arrays[n + bit]
                        swapped[n] = jnp.where(low, one, pltpu.roll(two, bit * 16, 1))
                        swapped[n + bit] = jnp.where(low, pltpu.roll(one, LANES - bit * 16, 1), two)
                arrays = swapped
            for n in range(8):
                z = (z_me + pair[n // 4]) & 7
                send_lat[c * LATS + (z << 2) + n % 4] = jnp.concatenate([arrays[n], no_rows], axis=0).astype(BF16)

        def relay(l, carry):
            z, x, c = (z_me + jnp.where(l & 4 == 0, pair[0], pair[1])) & 7, (x_me + l) & 3, (c_me + (l >> 3)) & 1
            a = (z << 2) + x

            @pl.when((a != a_me) | (c != c_me))
            def _():
                pltpu.make_async_remote_copy(
                    src_ref=send_lat.at[(c << 5) + a],
                    dst_ref=last.at[c_me, a_me],
                    send_sem=lat_send_sem,
                    recv_sem=lat_recv_sem.at[c_me],
                    device_id=(a, (y_me << 1) + c),
                    device_id_type=MESH,
                ).start()

            return carry

        lax.fori_loop(0, 16, relay, 0)
    last[c_me, a_me] = send_lat[(c_me << 5) + a_me]

    for core in range(2):
        for count in (LATS - 1, LATS):

            @pl.when(c_me == (core if count < LATS else 1 - core))
            def _():
                arrived = last.at[core, pl.ds(0, count)]
                pltpu.make_async_copy(arrived, arrived, lat_recv_sem.at[core]).wait()

        for a in range(LATS):
            at = ((a % 4) * 8 + a // 4) * RLEN
            dt[core, at : at + RLEN, :] = last[core, a].astype(F32)[:RLEN]
        for lt in range(LTILES):
            at = slice(lt * LANES, (lt + 1) * LANES)
            turned = jnp.transpose(dt[core, at, :])
            for p in range(2):
                weight = mw[p * 8 : p * 8 + 8, at]
                for b in range(core, LEVS, 2):
                    start = b // 2 * 16 + p * 8
                    both = [turned[comp * 64 + start : comp * 64 + start + 8] * weight for comp in range(2)]
                    dsp[p, b * 16 : b * 16 + 16, at] = jnp.concatenate(both, axis=0).astype(BF16)

    for p in range(2):
        product = lax.dot_general(leg[p], dsp[p], (((1,), (1,)), ((), ())), preferred_element_type=F32)
        for n in range(PAIRLEN // LANES):
            at = slice(n * LANES, (n + 1) * LANES)
            rs[n] = jnp.transpose(product[at])
            for c in range(2):
                total = None
                for par in range(2):
                    north = rs[n, pl.ds(c * 2 + par, 16, stride=8), :]
                    south = rs[n, pl.ds(4 + c * 2 + par, 16, stride=8), :]
                    term = masks[p][par][:, at] * (north + signs[p][par][:, at] * south)
                    total = term if total is None else total + term
                res[n, pl.ds(2 * c + p, 16, stride=4), :] = total

    for n in range(PAIRLEN // LANES):
        out[:, :, :, n * LANES : (n + 1) * LANES] = res[n].astype(BF16).reshape(16, 2, 2, LANES)
    pltpu.make_async_copy(recv.at[others], recv.at[others], send_sem).wait()
    sent = send_lev.at[:, pl.ds(0, 6)]
    pltpu.make_async_copy(sent, sent, lev_send_sem).wait()
    sent = send_lat.at[pl.ds(0, 2 * LATS - 1)]
    pltpu.make_async_copy(sent, sent, lat_send_sem).wait()


def on_device(table, coeffs, legendre, pair_first, row_counts, quad_weights):
    vmem = pl.BlockSpec(memory_space=pltpu.VMEM)
    hbm = pl.BlockSpec(memory_space=pltpu.HBM)
    result = pl.pallas_call(
        kernel,
        out_shape=jax.ShapeDtypeStruct((16, 2, 2, PAIRLEN), BF16),
        in_specs=[hbm] * 6,
        out_specs=vmem,
        scratch_shapes=[
            pltpu.VMEM((KIN, 2, 2, PAIRLEN), BF16),
            pltpu.VMEM((PAIRLEN // LANES, 4 * KIN, LANES), F32),
            pltpu.VMEM((PAIRLEN // LANES, 64, LANES), F32),
            pltpu.VMEM((HALF,), jnp.int32),
            pltpu.VMEM((2 * HLAT,), jnp.int32),
            pltpu.VMEM((HLAT,), F32),
            pltpu.VMEM((2, PAIRLEN, HLAT), BF16),
            pltpu.VMEM((HALF, 4 * JPAD), BF16),
            pltpu.VMEM((HALF, 4 * JPAD), BF16),
            pltpu.VMEM((LTILES, 384, LANES), F32),
            pltpu.VMEM((LATS, LEVS, 16, LANES), BF16),
            pltpu.VMEM((DEVICES, 16, LANES), BF16),
            pltpu.VMEM((DEVICES * 16, LANES), F32),
            pltpu.VMEM((4, 256, HALF), BF16),
            pltpu.VMEM((4, 256, JPAD), BF16),
            pltpu.VMEM((4, LEVS, 2 * RLEN, LANES), BF16),
            pltpu.VMEM((4, 2, 4, 2 * RLEN, LANES), BF16),
            pltpu.VMEM((2 * LATS, RLEN + 8, LANES), BF16),
            pltpu.VMEM((2, LATS, RLEN + 8, LANES), BF16),
            pltpu.VMEM((2, HLAT, LANES), F32),
            pltpu.VMEM((2, 128, HLAT), BF16),
            pltpu.VMEM((PAIRLEN // LANES, 128, LANES), F32),
            pltpu.VMEM((16, HLAT), F32),
            pltpu.SemaphoreType.DMA((4,)),
            pltpu.SemaphoreType.DMA,
            pltpu.SemaphoreType.DMA,
            pltpu.SemaphoreType.DMA,
            pltpu.SemaphoreType.DMA,
            pltpu.SemaphoreType.DMA,
            pltpu.SemaphoreType.DMA((4,)),
            pltpu.SemaphoreType.DMA,
            pltpu.SemaphoreType.DMA((2,)),
            pltpu.SemaphoreType.REGULAR((2,)),
            pltpu.SemaphoreType.DMA((4,)),
        ],
        compiler_params=pltpu.CompilerParams(
            collective_id=0, has_side_effects=True, vmem_limit_bytes=62 * 2**20
        ),
        name="transforms",
    )(coeffs, legendre, table, pair_first, row_counts, quad_weights)
    return result


def solution(mesh):
    placed = (P(None, None, ("lat", "lev"), None), P(("lat", "lev"), None, None), P(), P(), P())
    table = table_constant()
    return jax.shard_map(
        functools.partial(on_device, table),
        mesh=mesh,
        in_specs=placed,
        out_specs=P(None, None, ("lat", "lev"), None),
        check_vma=False,
    )
```
